32 devices in a mesh: sub: 16 (over z, y, x), rng: 2 (over core).
Axes of the slice: x: 2, y: 2, z: 4, core: 2. Of those that a mesh axis runs over, the one named last changes fastest.
Arguments:
- raw_echoes: bfloat16 [2048, 2, 16384], P('sub', None, 'rng'), may hold values from -6 to 6
- chirp_replica: bfloat16 [2, 512], replicated, may hold values from -0.1875 to 0.1875
- steering: bfloat16 [16, 2, 128, 128], P('sub'), may hold values from -0.375 to 0.375
- band_start: int32 [4, 16, 2, 128], P(None, 'sub'), may hold values from 0 to 120
- band_coef: bfloat16 [4, 16, 2, 2, 8, 128], P(None, 'sub'), may hold values from -1 to 1
- phase_rate: float32 [4, 16, 128], P(None, 'sub'), may hold values from -8 to 8
- range_map: bfloat16 [2, 8192, 256], P(None, 'rng'), may hold values from -0.0625 to 0.0625
- slot_maps: bfloat16 [512, 2, 32, 128], P(('sub', 'rng')), may hold values from -0.09375 to 0.09375
- coverage: int32 [512, 1], P(('sub', 'rng')), may hold values from 0 to 31, as said below
Outputs:
- ground_tiles: float32 [32, 2, 32, 256], P(('sub', 'rng'))
The draws below stay inside these ranges and needn't reach their ends.
Inputs may be any that keep to these rules, and one draw needn't show every extreme that they name: `coverage`: within the rows of one device (aligned blocks of 16 rows) no tile is named more than 2 times; in every block one tile is named exactly 2 times.
All inputs are finite; a program needn't handle non-finite values.
Results may differ from the reference program's by a relative error of at most 0.012.
Values may be sent and summed in bfloat16 or wider, within the bound.
A program may use at most 128 MiB of HBM per device.

```python
import math
import jax
import jax.numpy as jnp
from jax import lax

PULSES_DEV = 128
RANGE = 16384
CHIRP = 512
BEAMS = 128
BAND = 8
SECTIONS = 4
TB = 32
TR = 256
CAP = 2
SUBAPS = 16
PULSES = 2048
RBINS = 8192
RBLOCKS = 2
RBINS_DEV = 4096
TILES = 32
SLOTS = 16
SLOTS_ALL = 512
N_RNG = 2


def draw_coverage(key, part):
    hottest = jax.random.randint(jax.random.fold_in(key, 11), (), 0, TILES)
    popularity = jax.random.randint(jax.random.fold_in(key, 12), (TILES,), 0, 4)
    tile_ids = jnp.arange(TILES).astype(jnp.int32)

    def one_device(device_key):
        first_key, second_key, third_key = jax.random.split(device_key, 3)
        shuffled = jax.random.permutation(first_key, TILES).astype(jnp.int32)
        scores = (popularity * (TILES // 2) + shuffled) * TILES + shuffled
        scores = jnp.where(tile_ids == hottest, -1, scores)
        unused, picked = lax.top_k(scores, SLOTS - CAP)
        picked = picked.astype(jnp.int32)
        repeat_flag = jax.random.randint(second_key, (), 0, 2)
        last_entry = jnp.where(repeat_flag == 1, picked[0], picked[SLOTS - CAP - 1])
        picked = jnp.concatenate([picked[:SLOTS - CAP - 1], last_entry[None]])
        entries = jnp.concatenate([jnp.full((CAP,), hottest, jnp.int32), picked])
        ordering = jax.random.permutation(third_key, SLOTS)
        return entries[ordering]
    device_keys = jax.random.split(jax.random.fold_in(key, 13), TILES)
    return jax.vmap(one_device)(device_keys).reshape(SLOTS_ALL, 1).astype(jnp.int32)


def with_ends(values, stream_key, smallest, largest):
    shape = values.shape
    spot = [jax.random.randint(jax.random.fold_in(stream_key, axis), (), 0, shape[axis]) for axis in range(len(shape))]
    values = values.at[tuple(spot)].set(smallest)
    longest = shape.index(max(shape))
    spot[longest] = (spot[longest] + 1) % shape[longest]
    return values.at[tuple(spot)].set(largest)


def level_of(key, extent, cuts, least, top_value):
    gain = 1.0
    for axis_at, blocks in cuts:
        heights = jax.random.uniform(jax.random.fold_in(jax.random.fold_in(key, 6), axis_at), (blocks,), jnp.float32, least / len(cuts), top_value / len(cuts))
        gain = gain * jnp.repeat(jnp.exp(heights), extent[axis_at] // blocks).reshape((-1,) + (1,) * (len(extent) - 1 - axis_at))
    return gain


def gaussian(rng, shape, deviation, most, shards=(), kind=jnp.bfloat16):
    loudness = level_of(rng, shape, shards, -0.22, 0.18) if shards else 1.0
    result = jax.random.normal(rng, shape, jnp.float32) * deviation * loudness
    return jnp.minimum(jnp.maximum(result, -most), most).astype(kind)


def setup_inputs(seed: int = 0) -> dict:
    keys = jax.random.split(jax.random.key(seed), 10)
    return {
        "raw_echoes": gaussian(keys[0], (PULSES, 2, RANGE), 1.0, 6.0, ((0, 16), (2, 2))),
        "chirp_replica": gaussian(keys[1], (2, CHIRP), (2 * CHIRP) ** -0.5, 0.1875),
        "steering": gaussian(keys[2], (SUBAPS, 2, BEAMS, PULSES_DEV), (2 * PULSES_DEV) ** -0.5, 0.375, ((0, 16),)),
        "band_start": with_ends(jax.random.randint(keys[3], (SECTIONS, SUBAPS, 2, BEAMS), 0, BEAMS - BAND + 1), jax.random.fold_in(keys[3], 1), 0, BEAMS - BAND).astype(jnp.int32),
        "band_coef": gaussian(keys[4], (SECTIONS, SUBAPS, 2, 2, BAND, BEAMS), (4 * BAND) ** -0.5, 1.0, ((1, 16),)),
        "phase_rate": jnp.clip(jax.random.uniform(keys[5], (SECTIONS, SUBAPS, BEAMS), jnp.float32, -8.0, 8.0) * level_of(keys[5], (SECTIONS, SUBAPS, BEAMS), ((1, 16),), -0.4, 0.0), -8.0, 8.0),
        "range_map": gaussian(keys[6], (2, RBINS, TR), (2 * RBINS // N_RNG) ** -0.5, 0.0625, ((1, 2),)),
        "slot_maps": gaussian(keys[7], (SLOTS_ALL, 2, TB, BEAMS), (2 * BEAMS * SLOTS) ** -0.5, 0.09375, ((0, 32),)),
        "coverage": draw_coverage(jax.random.fold_in(keys[9], 71), 0),
    }


def toeplitz_taps(replica):
    quarter = CHIRP // 4
    window_width = 6 * quarter
    positions = jnp.arange(window_width).astype(jnp.int32)[:, None] - 2 * jnp.arange(quarter).astype(jnp.int32)[None, :]
    inside = (positions >= 0) & (positions < CHIRP)
    clipped = jnp.clip(positions, 0, CHIRP - 1)
    values = replica.astype(jnp.float32)[:, clipped]
    return jnp.where(inside[None], values, jnp.float32(0.0))


def compress(pulse_block, toeplitz):
    quarter = CHIRP // 4
    stride = 2 * quarter
    window_count = RANGE // stride
    data = pulse_block.astype(jnp.float32)
    pulses = data.shape[0]
    padded = jnp.concatenate([data, jnp.zeros((pulses, 2, CHIRP), jnp.float32)], axis=2)
    blocks = padded.reshape(pulses, 2, window_count + 2, stride)
    windows = jnp.concatenate([blocks[:, :, :window_count], blocks[:, :, 1:window_count + 1], blocks[:, :, 2:]], axis=3)
    products = jnp.einsum("pcnw,ewq->pcenq", windows, toeplitz)
    real_part = products[:, 0, 0] + products[:, 1, 1]
    imag_part = products[:, 1, 0] - products[:, 0, 1]
    return jnp.stack([real_part, imag_part], axis=1).reshape(pulses, 2, RBINS).astype(jnp.bfloat16)


def project(items):
    steer, pulse_rows = items
    products = jnp.einsum("cbp,pdr->cdbr", steer.astype(jnp.float32), pulse_rows.astype(jnp.float32))
    return jnp.stack([products[0, 0] - products[1, 1], products[0, 1] + products[1, 0]]).astype(jnp.bfloat16)


def band_apply(field, starts, coefs):
    rows = starts[:, None] + jnp.arange(BAND).astype(jnp.int32)[None, :]
    picked = field.astype(jnp.float32)[:, rows, :]
    coef_real = jnp.transpose(coefs[0].astype(jnp.float32))[:, :, None]
    coef_imag = jnp.transpose(coefs[1].astype(jnp.float32))[:, :, None]
    real_part = jnp.sum(coef_real * picked[0] - coef_imag * picked[1], axis=1)
    imag_part = jnp.sum(coef_real * picked[1] + coef_imag * picked[0], axis=1)
    return real_part, imag_part


def merge(items):
    own_image, partner_image, starts, coefs, rates = items
    own_real, own_imag = band_apply(own_image, starts[0], coefs[0])
    part_real, part_imag = band_apply(partner_image, starts[1], coefs[1])
    bins = jnp.arange(RBINS).astype(jnp.float32)
    angle = (rates.astype(jnp.float32)[:, None] * bins[None, :]) * (2.0 * math.pi / RBINS_DEV)
    cosine = jnp.cos(angle)
    sine = jnp.sin(angle)
    turned_real = part_real * cosine - part_imag * sine
    turned_imag = part_real * sine + part_imag * cosine
    return jnp.stack([own_real + turned_real, own_imag + turned_imag]).astype(jnp.bfloat16)


def reference(raw_echoes, chirp_replica, steering, band_start, band_coef, phase_rate, range_map, slot_maps, coverage):
    toeplitz = toeplitz_taps(chirp_replica)
    compressed = lax.map(lambda pulse_block: compress(pulse_block, toeplitz), raw_echoes.reshape(SUBAPS, PULSES_DEV, 2, RANGE))
    polar = lax.map(project, (steering, compressed))
    for section_bit in range(SECTIONS):
        group = 2 ** section_bit
        partner = polar.reshape(SUBAPS // (2 * group), 2, group, 2, BEAMS, RBINS)[:, ::-1].reshape(SUBAPS, 2, BEAMS, RBINS)
        polar = lax.map(merge, (polar, partner, band_start[section_bit], band_coef[section_bit], phase_rate[section_bit]))
    maps_float = range_map.astype(jnp.float32).reshape(2, RBLOCKS, RBINS_DEV, TR)

    def basis_of(polar_image):
        pieces = polar_image.astype(jnp.float32).reshape(2, BEAMS, RBLOCKS, RBINS_DEV)
        products = jnp.einsum("cbhr,dhrt->cdhbt", pieces, maps_float)
        stacked = jnp.stack([products[0, 0] - products[1, 1], products[0, 1] + products[1, 0]])
        return jnp.transpose(stacked, (1, 0, 2, 3)).astype(jnp.bfloat16)

    tile_basis = lax.map(basis_of, polar).reshape(TILES, 2, BEAMS, TR)

    def accumulate(total, items):
        basis, maps, targets = items
        products = jnp.einsum("kcab,dbt->kcdat", maps.astype(jnp.float32), basis.astype(jnp.float32))
        parts = jnp.stack([products[:, 0, 0] - products[:, 1, 1], products[:, 0, 1] + products[:, 1, 0]], axis=1).reshape(SLOTS, 2 * TB * TR)
        select = (jnp.arange(TILES).astype(jnp.int32)[:, None] == targets[None, :]).astype(jnp.float32)
        return total + jnp.dot(select, parts, precision=lax.Precision.HIGHEST, preferred_element_type=jnp.float32), None

    initial = jnp.zeros((TILES, 2 * TB * TR), jnp.float32)
    total, unused = lax.scan(accumulate, initial, (tile_basis, slot_maps.reshape(TILES, SLOTS, 2, TB, BEAMS), coverage.reshape(TILES, SLOTS)))
    return total.reshape(TILES, 2, TB, TR)
```

```python
import functools
import math

import jax
import jax.numpy as jnp
from jax import lax
from jax.experimental import pallas as pl
from jax.experimental.pallas import tpu as pltpu
from jax.sharding import PartitionSpec as P

LANES = 128
F32 = jnp.float32
BF16 = jnp.bfloat16
SLOT_BLOCK = 16


def mm(a, b):
    return jnp.dot(a, b, preferred_element_type=F32)


def from_behind(value, axis, steps):
    count = lax.axis_size(axis)
    initial, last = (max(0, -steps), min(count, count - steps))
    return lax.ppermute(value, axis, [(source, source + steps) for source in range(initial, last)])


def toeplitz_taps(replica, quarter, window_width):
    tap_count = replica.shape[1]
    period = window_width + 2
    padded = jnp.concatenate([replica, jnp.zeros((2, period - tap_count), replica.dtype)], axis=1)
    repeated = jnp.tile(padded, (1, quarter + 1))[:, : quarter * window_width]
    return jnp.transpose(repeated.reshape(2 * quarter, window_width))


def front_kernel(steer_ref, taps_ref, raw_ref, next_ref, halo_ref, out_ref):
    beams = out_ref.shape[0] // 2
    quarter = taps_ref.shape[1] // 2
    last = pl.program_id(0) == pl.num_programs(0) - 1
    steer = steer_ref[...]
    after = jnp.where(last, halo_ref[...], next_ref[...])
    here = mm(steer, raw_ref[...]).astype(BF16)
    beyond = mm(steer, after).astype(BF16)
    field = jnp.concatenate([here, beyond], axis=1)
    width = taps_ref.shape[0]
    stride = 2 * quarter
    for n in range(raw_ref.shape[1] // stride):
        both = mm(field[:, n * stride : n * stride + width], taps_ref[...])
        cols = pl.ds(n * quarter, quarter)
        out_ref[:beams, cols] = (both[:beams, :quarter] + both[beams:, quarter:]).astype(BF16)
        out_ref[beams:, cols] = (both[beams:, :quarter] - both[:beams, quarter:]).astype(BF16)


def front(steer, taps, raw, halo):
    rows, length = raw.shape
    reach = halo.shape[1]
    chunk = 2 * reach
    steps = length // chunk
    ahead = chunk // reach
    return pl.pallas_call(
        front_kernel,
        grid=(steps,),
        in_specs=[
            pl.BlockSpec(steer.shape, lambda i: (0, 0)),
            pl.BlockSpec(taps.shape, lambda i: (0, 0)),
            pl.BlockSpec((rows, chunk), lambda i: (0, i)),
            pl.BlockSpec(
                (rows, reach), lambda i: (0, jnp.minimum(ahead * (i + 1), ahead * steps - 1))
            ),
            pl.BlockSpec(halo.shape, lambda i: (0, 0)),
        ],
        out_specs=pl.BlockSpec((steer.shape[0], chunk // 2), lambda i: (0, i)),
        out_shape=jax.ShapeDtypeStruct((steer.shape[0], length // 2), BF16),
        compiler_params=pltpu.CompilerParams(vmem_limit_bytes=40 * 1024 * 1024),
        cost_estimate=pl.CostEstimate(
            flops=8 * 10**9, bytes_accessed=7 * 10**6, transcendentals=0
        ),
        name="front",
    )(steer, taps, raw, raw, halo)


def top_bit(e):
    return e.bit_length() - 1


def own_list(sections):
    return [
        (s, e) for e in range(2**sections) for s in range(top_bit(e) + 1, sections)
    ]


def matrices_kernel(sections, taps, pick_ref, data_ref, turn_ref, own_ref, built):
    beams = data_ref.shape[4]
    nodes = 2**sections
    rows = lax.broadcasted_iota(jnp.int32, (beams, beams), 0).astype(F32)

    def build(m, carry):
        at = (pick_ref[3 * m], pick_ref[3 * m + 1], pick_ref[3 * m + 2])
        offset = rows - data_ref[at + (slice(2 * taps, 2 * taps + 1), slice(None))]
        real = jnp.zeros((beams, beams), F32)
        imag = jnp.zeros((beams, beams), F32)
        for t in range(taps):
            hit = offset == t
            real = jnp.where(hit, data_ref[at + (slice(t, t + 1), slice(None))], real)
            imag = jnp.where(
                hit, data_ref[at + (slice(taps + t, taps + t + 1), slice(None))], imag
            )
        built[m, :beams, :beams] = real.astype(BF16)
        built[m, beams:, beams:] = real.astype(BF16)
        built[m, :beams, beams:] = imag.astype(BF16)
        built[m, beams:, :beams] = (-imag).astype(BF16)
        return carry

    lax.fori_loop(0, built.shape[0], build, 0)
    place = {key: nodes - 1 + n for n, key in enumerate(own_list(sections))}
    for e in range(nodes):
        chain = None
        for s in range(top_bit(e) + 1, sections):
            child = e | 2**s
            partner = built[child - 1]
            turned = partner.astype(F32) if chain is None else mm(chain, partner)
            turn_ref[child - 1] = turned.T.astype(BF16)
            own = built[place[(s, e)]]
            chain = own if chain is None else mm(chain, own).astype(BF16)
        if chain is not None:
            own_ref[e] = chain.astype(F32).T.astype(BF16)


def matrices(data, place, sections, taps):
    nodes = 2**sections
    beams = data.shape[4]
    wanted = [(e, top_bit(e), 1) for e in range(1, nodes)]
    wanted += [(e, s, 0) for s, e in own_list(sections)]
    picks = jnp.stack([jnp.stack([place ^ e, place * 0 + s, place * 0 + j]) for e, s, j in wanted])
    return pl.pallas_call(
        functools.partial(matrices_kernel, sections, taps),
        grid_spec=pltpu.PrefetchScalarGridSpec(
            num_scalar_prefetch=1,
            grid=(1,),
            in_specs=[pl.BlockSpec(data.shape, lambda i, p: (0,) * 5)],
            out_specs=(
                pl.BlockSpec((nodes - 1, 2 * beams, 2 * beams), lambda i, p: (0, 0, 0)),
                pl.BlockSpec((nodes // 2, 2 * beams, 2 * beams), lambda i, p: (0, 0, 0)),
            ),
            scratch_shapes=[pltpu.VMEM((len(wanted), 2 * beams, 2 * beams), BF16)],
        ),
        out_shape=(
            jax.ShapeDtypeStruct((nodes - 1, 2 * beams, 2 * beams), BF16),
            jax.ShapeDtypeStruct((nodes // 2, 2 * beams, 2 * beams), BF16),
        ),
        compiler_params=pltpu.CompilerParams(vmem_limit_bytes=40 * 1024 * 1024),
        cost_estimate=pl.CostEstimate(
            flops=5 * 10**9, bytes_accessed=5 * 10**6, transcendentals=0
        ),
        name="matrices",
    )(picks.reshape(-1), data)


def tree_kernel(
    sections, polar_ref, map_ref, turn_ref, own_ref, fine_ref, coarse_ref, out_ref, field, total
):
    step = pl.program_id(0)
    beams = polar_ref.shape[0] // 2
    width = polar_ref.shape[1]
    cols = map_ref.shape[2]
    nodes = 2**sections

    @pl.when(step == 0)
    def _():
        total[...] = jnp.zeros_like(total)

    def project(e, value):
        total[e, :, :cols] += mm(value, map_ref[0])
        total[e, :, cols:] += mm(value, map_ref[1])

    field[0] = polar_ref[...]
    project(0, polar_ref[...])
    for e in range(1, nodes):
        parent = e ^ (2 ** top_bit(e))
        merged = mm(turn_ref[e - 1], field[parent])
        fine_cos, fine_sin = fine_ref[e - 1, 0], fine_ref[e - 1, 1]
        for j in range(width // LANES):
            at = slice(j * LANES, (j + 1) * LANES)
            c = coarse_ref[0, e - 1, 0, :, j : j + 1]
            s = coarse_ref[0, e - 1, 1, :, j : j + 1]
            cosine = fine_cos * c - fine_sin * s
            sine = fine_cos * s + fine_sin * c
            real, imag = merged[:beams, at], merged[beams:, at]
            field[e, :beams, at] = (real * cosine - imag * sine).astype(BF16)
            field[e, beams:, at] = (real * sine + imag * cosine).astype(BF16)
        project(e, field[e])

    @pl.when(step == pl.num_programs(0) - 1)
    def _():
        for e in range(nodes):
            real = total[e, :beams, :cols] - total[e, beams:, cols:]
            imag = total[e, :beams, cols:] + total[e, beams:, :cols]
            basis = jnp.concatenate([real, imag], axis=0).astype(BF16)
            if e < nodes // 2:
                basis = mm(own_ref[e], basis).astype(BF16)
            out_ref[e] = basis


def tree(polar, range_map, turn, own, fine, coarse, sections):
    rows, bins = polar.shape
    cols = range_map.shape[2]
    nodes = 2**sections
    chunk = coarse.shape[4] * LANES
    whole = lambda array: pl.BlockSpec(array.shape, lambda i: (0,) * array.ndim)
    return pl.pallas_call(
        functools.partial(tree_kernel, sections),
        grid=(bins // chunk,),
        in_specs=[
            pl.BlockSpec((rows, chunk), lambda i: (0, i)),
            pl.BlockSpec((2, chunk, cols), lambda i: (0, i, 0)),
            whole(turn),
            whole(own),
            whole(fine),
            pl.BlockSpec((1,) + coarse.shape[1:], lambda i: (i, 0, 0, 0, 0)),
        ],
        out_specs=pl.BlockSpec((nodes, rows, cols), lambda i: (0, 0, 0)),
        out_shape=jax.ShapeDtypeStruct((nodes, rows, cols), BF16),
        scratch_shapes=[
            pltpu.VMEM((nodes, rows, chunk), BF16),
            pltpu.VMEM((nodes, rows, 2 * cols), F32),
        ],
        compiler_params=pltpu.CompilerParams(vmem_limit_bytes=52 * 1024 * 1024),
        cost_estimate=pl.CostEstimate(
            flops=40 * 10**9, bytes_accessed=12 * 10**6, transcendentals=0
        ),
        name="tree",
    )(polar, range_map, turn, own, fine, coarse)


def tiles_kernel(slots, place_ref, cover_ref, basis_ref, maps_ref, out_ref):
    e, block = pl.program_id(0), pl.program_id(1)

    @pl.when((e == 0) & (block == 0))
    def _():
        out_ref[...] = jnp.zeros_like(out_ref)

    count, _, rows, beams = maps_ref.shape[1:]
    real = maps_ref[0, :, 0].reshape(count * rows, beams)
    imag = maps_ref[0, :, 1].reshape(count * rows, beams)
    basis = basis_ref[0]
    part_real = mm(jnp.concatenate([real, -imag], axis=1), basis)
    part_imag = mm(jnp.concatenate([imag, real], axis=1), basis)
    first = (place_ref[0] ^ e) * slots + block * count
    for k in range(count):
        tile = cover_ref[first + k]
        out_ref[tile, 0] += part_real[k * rows : (k + 1) * rows]
        out_ref[tile, 1] += part_imag[k * rows : (k + 1) * rows]


def tiles(place, cover, basis, maps, tile_count):
    nodes, slots, _, rows, beams = maps.shape
    block = math.gcd(slots, SLOT_BLOCK)
    cols = basis.shape[2]
    shape = (tile_count, 2, rows, cols)
    return pl.pallas_call(
        functools.partial(tiles_kernel, slots),
        grid_spec=pltpu.PrefetchScalarGridSpec(
            num_scalar_prefetch=2,
            grid=(nodes, slots // block),
            in_specs=[
                pl.BlockSpec((1,) + basis.shape[1:], lambda e, k, p, c: (e, 0, 0)),
                pl.BlockSpec(
                    (1, block, 2, rows, beams), lambda e, k, p, c: (p[0] ^ e, k, 0, 0, 0)
                ),
            ],
            out_specs=pl.BlockSpec(shape, lambda e, k, p, c: (0, 0, 0, 0)),
        ),
        out_shape=jax.ShapeDtypeStruct(shape, F32),
        compiler_params=pltpu.CompilerParams(vmem_limit_bytes=40 * 1024 * 1024),
        cost_estimate=pl.CostEstimate(
            flops=5 * 10**9, bytes_accessed=9 * 10**6, transcendentals=0
        ),
        name="tiles",
    )(place, cover, basis, maps)


def shards(
    raw_echoes,
    chirp_replica,
    steering,
    band_start,
    band_coef,
    phase_rate,
    range_map,
    slot_maps,
    coverage,
):
    pulses, _, range_len = raw_echoes.shape
    tap_count = chirp_replica.shape[1]
    quarter = tap_count // 4
    sections, _, _, _, band, beams = band_coef.shape
    nodes = 2**sections
    subs = lax.axis_size("sub")
    owners = subs * lax.axis_size("rng")
    slot_count = slot_maps.shape[0]
    bins = range_len // 2
    groups = None
    if subs != nodes:
        groups = [list(range(g, g + nodes)) for g in range(0, subs, nodes)]
    place = lax.axis_index("sub") % nodes

    everywhere = (sections, 2, 1, beams)
    cover_row = jnp.pad(coverage[:, 0].astype(F32), (0, beams - slot_count))
    packed = jnp.concatenate(
        [
            band_coef[:, 0].astype(F32).reshape(sections, 2, 2 * band, beams),
            band_start[:, 0].astype(F32)[:, :, None],
            jnp.broadcast_to(phase_rate[:, 0][:, None, None], everywhere),
            jnp.broadcast_to(cover_row, everywhere),
        ],
        axis=2,
    )
    gathered = lax.all_gather(packed, "sub", axis_index_groups=groups)
    maps = lax.all_gather(slot_maps, "sub", axis_index_groups=groups)
    cover = gathered[:, 0, 0, 2 * band + 2, :slot_count].reshape(-1).astype(jnp.int32)
    turn, own = matrices(gathered, place, sections, band)
    rates = gathered[:, :, 1, 2 * band + 1]
    ids = jnp.arange(nodes)
    rate = jnp.stack(
        [
            jnp.sum(jnp.where((ids == place ^ e)[:, None], rates[:, top_bit(e)], 0.0), axis=0)
            for e in range(1, nodes)
        ]
    )
    unit = 2.0 * math.pi / bins
    lane = lax.iota(jnp.int32, LANES).astype(F32)
    chunk = 512
    first = (
        lax.axis_index("rng") * bins + lax.iota(jnp.int32, bins // LANES) * LANES
    ).astype(F32)
    fine_angle = rate[:, :, None] * lane * unit
    fine = jnp.stack([jnp.cos(fine_angle), jnp.sin(fine_angle)], axis=1)
    coarse_angle = rate[:, :, None] * first * unit
    coarse = jnp.stack([jnp.cos(coarse_angle), jnp.sin(coarse_angle)], axis=1)
    coarse = coarse.reshape(nodes - 1, 2, beams, bins // chunk, chunk // LANES)
    coarse = jnp.transpose(coarse, (3, 0, 1, 2, 4))

    raw = raw_echoes.reshape(2 * pulses, range_len)
    halo = from_behind(raw_echoes[:, :, :tap_count], "rng", -1).reshape(2 * pulses, tap_count)
    taps = toeplitz_taps(chirp_replica, quarter, 6 * quarter)
    taps = taps.reshape(6 * quarter, 2 * quarter)
    real, imag = steering[0, 0], steering[0, 1]
    steer = jnp.concatenate(
        [
            jnp.stack([real, -imag], axis=2).reshape(beams, 2 * pulses),
            jnp.stack([imag, real], axis=2).reshape(beams, 2 * pulses),
        ],
        axis=0,
    )
    polar = front(steer, taps, raw, halo)
    basis = tree(polar, range_map, turn, own, fine, coarse, sections)
    partial = tiles(place.reshape(1), cover, basis, maps, owners)
    return lax.psum_scatter(partial, ("sub", "rng"), scatter_dimension=0, tiled=True)


def solution(mesh):
    in_specs = (
        P("sub", None, "rng"),
        P(),
        P("sub", None, None, None),
        P(None, "sub", None, None),
        P(None, "sub", None, None, None, None),
        P(None, "sub", None),
        P(None, "rng", None),
        P(("sub", "rng"), None, None, None),
        P(("sub", "rng"), None),
    )
    out_specs = P(("sub", "rng"), None, None, None)
    return jax.shard_map(shards, mesh=mesh, in_specs=in_specs, out_specs=out_specs, check_vma=False)
```

```python
import functools
import math

import jax
import jax.numpy as jnp
from jax import lax
from jax.experimental import pallas as pl
from jax.experimental.pallas import tpu as pltpu
from jax.sharding import PartitionSpec as P

LANES = 128
F32 = jnp.float32
BF16 = jnp.bfloat16
SLOT_BLOCK = 16


def mm(a, b):
    return jnp.dot(a, b, preferred_element_type=F32)


def from_behind(value, axis, steps):
    count = lax.axis_size(axis)
    initial, last = (max(0, -steps), min(count, count - steps))
    return lax.ppermute(value, axis, [(source, source + steps) for source in range(initial, last)])


def swapped(value, axis, distance):
    mask = 2**distance
    pairs = [(source, source ^ mask) for source in range(lax.axis_size(axis))]
    return lax.ppermute(value, axis, pairs)


def toeplitz_taps(replica, quarter, window_width):
    tap_count = replica.shape[1]
    period = window_width + 2
    padded = jnp.concatenate([replica, jnp.zeros((2, period - tap_count), replica.dtype)], axis=1)
    repeated = jnp.tile(padded, (1, quarter + 1))[:, : quarter * window_width]
    return jnp.transpose(repeated.reshape(2 * quarter, window_width))


def front_kernel(steer_ref, taps_ref, raw_ref, next_ref, halo_ref, out_ref):
    beams = out_ref.shape[0] // 2
    quarter = taps_ref.shape[1] // 2
    last = pl.program_id(0) == pl.num_programs(0) - 1
    steer = steer_ref[...]
    after = jnp.where(last, halo_ref[...], next_ref[...])
    here = mm(steer, raw_ref[...]).astype(BF16)
    beyond = mm(steer, after).astype(BF16)
    field = jnp.concatenate([here, beyond], axis=1)
    width = taps_ref.shape[0]
    stride = 2 * quarter
    for n in range(raw_ref.shape[1] // stride):
        both = mm(field[:, n * stride : n * stride + width], taps_ref[...])
        cols = pl.ds(n * quarter, quarter)
        out_ref[:beams, cols] = (both[:beams, :quarter] + both[beams:, quarter:]).astype(BF16)
        out_ref[beams:, cols] = (both[beams:, :quarter] - both[:beams, quarter:]).astype(BF16)


def front(steer, taps, raw, halo):
    rows, length = raw.shape
    reach = halo.shape[1]
    chunk = 2 * reach
    steps = length // chunk
    ahead = chunk // reach
    return pl.pallas_call(
        front_kernel,
        grid=(steps,),
        in_specs=[
            pl.BlockSpec(steer.shape, lambda i: (0, 0)),
            pl.BlockSpec(taps.shape, lambda i: (0, 0)),
            pl.BlockSpec((rows, chunk), lambda i: (0, i)),
            pl.BlockSpec(
                (rows, reach), lambda i: (0, jnp.minimum(ahead * (i + 1), ahead * steps - 1))
            ),
            pl.BlockSpec(halo.shape, lambda i: (0, 0)),
        ],
        out_specs=pl.BlockSpec((steer.shape[0], chunk // 2), lambda i: (0, i)),
        out_shape=jax.ShapeDtypeStruct((steer.shape[0], length // 2), BF16),
        compiler_params=pltpu.CompilerParams(vmem_limit_bytes=40 * 1024 * 1024),
        cost_estimate=pl.CostEstimate(
            flops=8 * 10**9, bytes_accessed=7 * 10**6, transcendentals=0
        ),
        name="front",
    )(steer, taps, raw, raw, halo)


def top_bit(e):
    return e.bit_length() - 1


def own_list(sections):
    return [
        (s, e) for e in range(2**sections) for s in range(top_bit(e) + 1, sections)
    ]


def matrices_kernel(sections, taps, pick_ref, data_ref, turn_ref, own_ref, built):
    beams = data_ref.shape[4]
    nodes = 2**sections
    rows = lax.broadcasted_iota(jnp.int32, (beams, beams), 0).astype(F32)

    def build(m, carry):
        at = (pick_ref[3 * m], pick_ref[3 * m + 1], pick_ref[3 * m + 2])
        offset = rows - data_ref[at + (slice(2 * taps, 2 * taps + 1), slice(None))]
        real = jnp.zeros((beams, beams), F32)
        imag = jnp.zeros((beams, beams), F32)
        for t in range(taps):
            hit = offset == t
            real = jnp.where(hit, data_ref[at + (slice(t, t + 1), slice(None))], real)
            imag = jnp.where(
                hit, data_ref[at + (slice(taps + t, taps + t + 1), slice(None))], imag
            )
        built[m, :beams, :beams] = real.astype(BF16)
        built[m, beams:, beams:] = real.astype(BF16)
        built[m, :beams, beams:] = imag.astype(BF16)
        built[m, beams:, :beams] = (-imag).astype(BF16)
        return carry

    lax.fori_loop(0, built.shape[0], build, 0)
    place = {key: nodes - 1 + n for n, key in enumerate(own_list(sections))}
    for e in range(nodes):
        chain = None
        for s in range(top_bit(e) + 1, sections):
            child = e | 2**s
            partner = built[child - 1]
            turned = partner.astype(F32) if chain is None else mm(chain, partner)
            turn_ref[child - 1] = turned.T.astype(BF16)
            own = built[place[(s, e)]]
            chain = own if chain is None else mm(chain, own).astype(BF16)
        if chain is not None:
            own_ref[e] = chain.astype(F32).T.astype(BF16)


def matrices(data, spot, sections, taps):
    nodes = 2**sections
    beams = data.shape[4]
    wanted = [(e, top_bit(e), 1) for e in range(1, nodes)]
    wanted += [(e, s, 0) for s, e in own_list(sections)]
    picks = jnp.array([[spot[e], s, j] for e, s, j in wanted], jnp.int32)
    return pl.pallas_call(
        functools.partial(matrices_kernel, sections, taps),
        grid_spec=pltpu.PrefetchScalarGridSpec(
            num_scalar_prefetch=1,
            grid=(1,),
            in_specs=[pl.BlockSpec(data.shape, lambda i, p: (0,) * 5)],
            out_specs=(
                pl.BlockSpec((nodes - 1, 2 * beams, 2 * beams), lambda i, p: (0, 0, 0)),
                pl.BlockSpec((nodes // 2, 2 * beams, 2 * beams), lambda i, p: (0, 0, 0)),
            ),
            scratch_shapes=[pltpu.VMEM((len(wanted), 2 * beams, 2 * beams), BF16)],
        ),
        out_shape=(
            jax.ShapeDtypeStruct((nodes - 1, 2 * beams, 2 * beams), BF16),
            jax.ShapeDtypeStruct((nodes // 2, 2 * beams, 2 * beams), BF16),
        ),
        compiler_params=pltpu.CompilerParams(vmem_limit_bytes=40 * 1024 * 1024),
        cost_estimate=pl.CostEstimate(
            flops=5 * 10**9, bytes_accessed=5 * 10**6, transcendentals=0
        ),
        name="matrices",
    )(picks.reshape(-1), data)


def tree_kernel(
    sections, polar_ref, map_ref, turn_ref, own_ref, fine_ref, coarse_ref, out_ref, field, total
):
    step = pl.program_id(0)
    beams = polar_ref.shape[0] // 2
    width = polar_ref.shape[1]
    cols = map_ref.shape[2]
    nodes = 2**sections

    @pl.when(step == 0)
    def _():
        total[...] = jnp.zeros_like(total)

    def project(e, value):
        total[e, :, :cols] += mm(value, map_ref[0])
        total[e, :, cols:] += mm(value, map_ref[1])

    field[0] = polar_ref[...]
    project(0, polar_ref[...])
    for e in range(1, nodes):
        parent = e ^ (2 ** top_bit(e))
        merged = mm(turn_ref[e - 1], field[parent])
        fine_cos, fine_sin = fine_ref[e - 1, 0], fine_ref[e - 1, 1]
        for j in range(width // LANES):
            at = slice(j * LANES, (j + 1) * LANES)
            c = coarse_ref[0, e - 1, 0, :, j : j + 1]
            s = coarse_ref[0, e - 1, 1, :, j : j + 1]
            cosine = fine_cos * c - fine_sin * s
            sine = fine_cos * s + fine_sin * c
            real, imag = merged[:beams, at], merged[beams:, at]
            field[e, :beams, at] = (real * cosine - imag * sine).astype(BF16)
            field[e, beams:, at] = (real * sine + imag * cosine).astype(BF16)
        project(e, field[e])

    @pl.when(step == pl.num_programs(0) - 1)
    def _():
        for e in range(nodes):
            real = total[e, :beams, :cols] - total[e, beams:, cols:]
            imag = total[e, :beams, cols:] + total[e, beams:, :cols]
            basis = jnp.concatenate([real, imag], axis=0).astype(BF16)
            if e < nodes // 2:
                basis = mm(own_ref[e], basis).astype(BF16)
            out_ref[e] = basis


def tree(polar, range_map, turn, own, fine, coarse, sections):
    rows, bins = polar.shape
    cols = range_map.shape[2]
    nodes = 2**sections
    chunk = coarse.shape[4] * LANES
    whole = lambda array: pl.BlockSpec(array.shape, lambda i: (0,) * array.ndim)
    return pl.pallas_call(
        functools.partial(tree_kernel, sections),
        grid=(bins // chunk,),
        in_specs=[
            pl.BlockSpec((rows, chunk), lambda i: (0, i)),
            pl.BlockSpec((2, chunk, cols), lambda i: (0, i, 0)),
            whole(turn),
            whole(own),
            whole(fine),
            pl.BlockSpec((1,) + coarse.shape[1:], lambda i: (i, 0, 0, 0, 0)),
        ],
        out_specs=pl.BlockSpec((nodes, rows, cols), lambda i: (0, 0, 0)),
        out_shape=jax.ShapeDtypeStruct((nodes, rows, cols), BF16),
        scratch_shapes=[
            pltpu.VMEM((nodes, rows, chunk), BF16),
            pltpu.VMEM((nodes, rows, 2 * cols), F32),
        ],
        compiler_params=pltpu.CompilerParams(vmem_limit_bytes=52 * 1024 * 1024),
        cost_estimate=pl.CostEstimate(
            flops=40 * 10**9, bytes_accessed=12 * 10**6, transcendentals=0
        ),
        name="tree",
    )(polar, range_map, turn, own, fine, coarse)


def tiles_kernel(slots, place_ref, cover_ref, basis_ref, maps_ref, out_ref):
    e, block = pl.program_id(0), pl.program_id(1)

    @pl.when((e == 0) & (block == 0))
    def _():
        out_ref[...] = jnp.zeros_like(out_ref)

    count, _, rows, beams = maps_ref.shape[1:]
    real = maps_ref[0, :, 0].reshape(count * rows, beams)
    imag = maps_ref[0, :, 1].reshape(count * rows, beams)
    basis = basis_ref[0]
    part_real = mm(jnp.concatenate([real, -imag], axis=1), basis)
    part_imag = mm(jnp.concatenate([imag, real], axis=1), basis)
    first = e * slots + block * count
    for k in range(count):
        tile = cover_ref[first + k]
        out_ref[tile, 0] += part_real[k * rows : (k + 1) * rows]
        out_ref[tile, 1] += part_imag[k * rows : (k + 1) * rows]


def tiles(place, cover, basis, maps, tile_count):
    nodes, slots, _, rows, beams = maps.shape
    block = math.gcd(slots, SLOT_BLOCK)
    cols = basis.shape[2]
    shape = (tile_count, 2, rows, cols)
    return pl.pallas_call(
        functools.partial(tiles_kernel, slots),
        grid_spec=pltpu.PrefetchScalarGridSpec(
            num_scalar_prefetch=2,
            grid=(nodes, slots // block),
            in_specs=[
                pl.BlockSpec((1,) + basis.shape[1:], lambda e, k, p, c: (e, 0, 0)),
                pl.BlockSpec(
                    (1, block, 2, rows, beams), lambda e, k, p, c: (p[0] ^ e, k, 0, 0, 0)
                ),
            ],
            out_specs=pl.BlockSpec(shape, lambda e, k, p, c: (0, 0, 0, 0)),
        ),
        out_shape=jax.ShapeDtypeStruct(shape, F32),
        compiler_params=pltpu.CompilerParams(vmem_limit_bytes=40 * 1024 * 1024),
        cost_estimate=pl.CostEstimate(
            flops=5 * 10**9, bytes_accessed=9 * 10**6, transcendentals=0
        ),
        name="tiles",
    )(place, cover, basis, maps)


def shards(
    raw_echoes,
    chirp_replica,
    steering,
    band_start,
    band_coef,
    phase_rate,
    range_map,
    slot_maps,
    coverage,
):
    pulses, _, range_len = raw_echoes.shape
    tap_count = chirp_replica.shape[1]
    quarter = tap_count // 4
    sections, _, _, _, band, beams = band_coef.shape
    nodes = 2**sections
    subs = lax.axis_size("sub")
    owners = subs * lax.axis_size("rng")
    slot_count = slot_maps.shape[0]
    bins = range_len // 2
    groups = None
    if subs != nodes:
        groups = [list(range(g, g + nodes)) for g in range(0, subs, nodes)]
    place = lax.axis_index("sub") % nodes

    everywhere = (sections, 2, 1, beams)
    cover_row = jnp.pad(coverage[:, 0].astype(F32), (0, beams - slot_count))
    packed = jnp.concatenate(
        [
            band_coef[:, 0].astype(F32).reshape(sections, 2, 2 * band, beams),
            band_start[:, 0].astype(F32)[:, :, None],
            jnp.broadcast_to(phase_rate[:, 0][:, None, None], everywhere),
            jnp.broadcast_to(cover_row, everywhere),
        ],
        axis=2,
    )
    relative = packed[None]
    for bit in reversed(range(sections)):
        relative = jnp.concatenate([relative, swapped(relative, "sub", bit)], axis=0)
    spot = [sum(((e >> b) & 1) << (sections - 1 - b) for b in range(sections)) for e in range(nodes)]
    maps = lax.all_gather(slot_maps, "sub", axis_index_groups=groups)
    cover = jnp.concatenate([relative[n, 0, 0, 2 * band + 2, :slot_count] for n in spot])
    cover = cover.astype(jnp.int32)
    turn, own = matrices(relative, spot, sections, band)
    rate = jnp.stack(
        [relative[spot[e], top_bit(e), 1, 2 * band + 1] for e in range(1, nodes)]
    )
    unit = 2.0 * math.pi / bins
    lane = lax.iota(jnp.int32, LANES).astype(F32)
    chunk = 512
    first = (
        lax.axis_index("rng") * bins + lax.iota(jnp.int32, bins // LANES) * LANES
    ).astype(F32)
    fine_angle = rate[:, :, None] * lane * unit
    fine = jnp.stack([jnp.cos(fine_angle), jnp.sin(fine_angle)], axis=1)
    coarse_angle = rate[:, :, None] * first * unit
    coarse = jnp.stack([jnp.cos(coarse_angle), jnp.sin(coarse_angle)], axis=1)
    coarse = coarse.reshape(nodes - 1, 2, beams, bins // chunk, chunk // LANES)
    coarse = jnp.transpose(coarse, (3, 0, 1, 2, 4))

    raw = raw_echoes.reshape(2 * pulses, range_len)
    halo = from_behind(raw_echoes[:, :, :tap_count], "rng", -1).reshape(2 * pulses, tap_count)
    taps = toeplitz_taps(chirp_replica, quarter, 6 * quarter)
    taps = taps.reshape(6 * quarter, 2 * quarter)
    real, imag = steering[0, 0], steering[0, 1]
    steer = jnp.concatenate(
        [
            jnp.stack([real, -imag], axis=2).reshape(beams, 2 * pulses),
            jnp.stack([imag, real], axis=2).reshape(beams, 2 * pulses),
        ],
        axis=0,
    )
    polar = front(steer, taps, raw, halo)
    basis = tree(polar, range_map, turn, own, fine, coarse, sections)
    partial = tiles(place.reshape(1), cover, basis, maps, owners)
    cores = lax.axis_size("rng")
    partial = partial.reshape((subs, cores) + partial.shape[1:])
    core = lax.axis_index("rng")
    half = lax.dynamic_index_in_dim(partial, core, 1, keepdims=False)
    for step in range(1, cores):
        away = lax.dynamic_index_in_dim(partial, (core + step) % cores, 1, keepdims=False)
        pairs = [(c, (c + step) % cores) for c in range(cores)]
        half = half + lax.ppermute(away.astype(BF16), "rng", pairs).astype(F32)
    received = lax.all_to_all(half.astype(BF16), "sub", split_axis=0, concat_axis=0, tiled=True)
    return jnp.sum(received.astype(F32), axis=0, keepdims=True)


def solution(mesh):
    in_specs = (
        P("sub", None, "rng"),
        P(),
        P("sub", None, None, None),
        P(None, "sub", None, None),
        P(None, "sub", None, None, None, None),
        P(None, "sub", None),
        P(None, "rng", None),
        P(("sub", "rng"), None, None, None),
        P(("sub", "rng"), None),
    )
    out_specs = P(("sub", "rng"), None, None, None)
    return jax.shard_map(shards, mesh=mesh, in_specs=in_specs, out_specs=out_specs, check_vma=False)
```

```python
import functools
import math

import jax
import jax.numpy as jnp
from jax import lax
from jax.experimental import pallas as pl
from jax.experimental.pallas import tpu as pltpu
from jax.sharding import PartitionSpec as P

LANES = 128
F32 = jnp.float32
BF16 = jnp.bfloat16
SLOT_BLOCK = 16


def mm(a, b):
    return jnp.dot(a, b, preferred_element_type=F32)


def from_behind(value, axis, steps):
    count = lax.axis_size(axis)
    initial, last = (max(0, -steps), min(count, count - steps))
    return lax.ppermute(value, axis, [(source, source + steps) for source in range(initial, last)])


def swapped(value, axis, distance):
    mask = 2**distance
    pairs = [(source, source ^ mask) for source in range(lax.axis_size(axis))]
    return lax.ppermute(value, axis, pairs)


def toeplitz_taps(replica, quarter, window_width):
    tap_count = replica.shape[1]
    period = window_width + 2
    padded = jnp.concatenate([replica, jnp.zeros((2, period - tap_count), replica.dtype)], axis=1)
    repeated = jnp.tile(padded, (1, quarter + 1))[:, : quarter * window_width]
    return jnp.transpose(repeated.reshape(2 * quarter, window_width))


def front_kernel(steer_ref, taps_ref, raw_ref, next_ref, halo_ref, out_ref):
    beams = out_ref.shape[0] // 2
    quarter = taps_ref.shape[1] // 2
    last = pl.program_id(0) == pl.num_programs(0) - 1
    steer = steer_ref[...]
    after = jnp.where(last, halo_ref[...], next_ref[...])
    here = mm(steer, raw_ref[...]).astype(BF16)
    beyond = mm(steer, after).astype(BF16)
    field = jnp.concatenate([here, beyond], axis=1)
    width = taps_ref.shape[0]
    stride = 2 * quarter
    for n in range(raw_ref.shape[1] // stride):
        both = mm(field[:, n * stride : n * stride + width], taps_ref[...])
        cols = pl.ds(n * quarter, quarter)
        out_ref[:beams, cols] = (both[:beams, :quarter] + both[beams:, quarter:]).astype(BF16)
        out_ref[beams:, cols] = (both[beams:, :quarter] - both[:beams, quarter:]).astype(BF16)


def front(steer, taps, raw, halo):
    rows, length = raw.shape
    reach = halo.shape[1]
    chunk = 2 * reach
    steps = length // chunk
    ahead = chunk // reach
    return pl.pallas_call(
        front_kernel,
        grid=(steps,),
        in_specs=[
            pl.BlockSpec(steer.shape, lambda i: (0, 0)),
            pl.BlockSpec(taps.shape, lambda i: (0, 0)),
            pl.BlockSpec((rows, chunk), lambda i: (0, i)),
            pl.BlockSpec(
                (rows, reach), lambda i: (0, jnp.minimum(ahead * (i + 1), ahead * steps - 1))
            ),
            pl.BlockSpec(halo.shape, lambda i: (0, 0)),
        ],
        out_specs=pl.BlockSpec((steer.shape[0], chunk // 2), lambda i: (0, i)),
        out_shape=jax.ShapeDtypeStruct((steer.shape[0], length // 2), BF16),
        compiler_params=pltpu.CompilerParams(vmem_limit_bytes=40 * 1024 * 1024),
        cost_estimate=pl.CostEstimate(
            flops=8 * 10**9, bytes_accessed=7 * 10**6, transcendentals=0
        ),
        name="front",
    )(steer, taps, raw, raw, halo)


def top_bit(e):
    return e.bit_length() - 1


def own_list(sections):
    return [
        (s, e) for e in range(2**sections) for s in range(top_bit(e) + 1, sections)
    ]


def matrices_kernel(sections, taps, pick_ref, data_ref, turn_ref, own_ref, built):
    beams = data_ref.shape[4]
    nodes = 2**sections
    rows = lax.broadcasted_iota(jnp.int32, (beams, beams), 0).astype(F32)

    def build(m, carry):
        at = (pick_ref[3 * m], pick_ref[3 * m + 1], pick_ref[3 * m + 2])
        offset = rows - data_ref[at + (slice(2 * taps, 2 * taps + 1), slice(None))]
        real = jnp.zeros((beams, beams), F32)
        imag = jnp.zeros((beams, beams), F32)
        for t in range(taps):
            hit = offset == t
            real = jnp.where(hit, data_ref[at + (slice(t, t + 1), slice(None))], real)
            imag = jnp.where(
                hit, data_ref[at + (slice(taps + t, taps + t + 1), slice(None))], imag
            )
        built[m, :beams, :beams] = real.astype(BF16)
        built[m, beams:, beams:] = real.astype(BF16)
        built[m, :beams, beams:] = imag.astype(BF16)
        built[m, beams:, :beams] = (-imag).astype(BF16)
        return carry

    lax.fori_loop(0, built.shape[0], build, 0)
    place = {key: nodes - 1 + n for n, key in enumerate(own_list(sections))}
    for e in range(nodes):
        chain = None
        for s in range(top_bit(e) + 1, sections):
            child = e | 2**s
            partner = built[child - 1]
            turned = partner.astype(F32) if chain is None else mm(chain, partner)
            turn_ref[child - 1] = turned.T.astype(BF16)
            own = built[place[(s, e)]]
            chain = own if chain is None else mm(chain, own).astype(BF16)
        if chain is not None:
            own_ref[e] = chain.astype(F32).T.astype(BF16)


def matrices(data, spot, sections, taps):
    nodes = 2**sections
    beams = data.shape[4]
    wanted = [(e, top_bit(e), 1) for e in range(1, nodes)]
    wanted += [(e, s, 0) for s, e in own_list(sections)]
    picks = jnp.array([[spot[e], s, j] for e, s, j in wanted], jnp.int32)
    return pl.pallas_call(
        functools.partial(matrices_kernel, sections, taps),
        grid_spec=pltpu.PrefetchScalarGridSpec(
            num_scalar_prefetch=1,
            grid=(1,),
            in_specs=[pl.BlockSpec(data.shape, lambda i, p: (0,) * 5)],
            out_specs=(
                pl.BlockSpec((nodes - 1, 2 * beams, 2 * beams), lambda i, p: (0, 0, 0)),
                pl.BlockSpec((nodes // 2, 2 * beams, 2 * beams), lambda i, p: (0, 0, 0)),
            ),
            scratch_shapes=[pltpu.VMEM((len(wanted), 2 * beams, 2 * beams), BF16)],
        ),
        out_shape=(
            jax.ShapeDtypeStruct((nodes - 1, 2 * beams, 2 * beams), BF16),
            jax.ShapeDtypeStruct((nodes // 2, 2 * beams, 2 * beams), BF16),
        ),
        compiler_params=pltpu.CompilerParams(vmem_limit_bytes=40 * 1024 * 1024),
        cost_estimate=pl.CostEstimate(
            flops=5 * 10**9, bytes_accessed=5 * 10**6, transcendentals=0
        ),
        name="matrices",
    )(picks.reshape(-1), data)


def tree_kernel(
    sections, polar_ref, map_ref, turn_ref, own_ref, fine_ref, coarse_ref, out_ref, field, total
):
    step = pl.program_id(0)
    beams = polar_ref.shape[0] // 2
    width = polar_ref.shape[1]
    cols = map_ref.shape[2]
    nodes = 2**sections

    @pl.when(step == 0)
    def _():
        total[...] = jnp.zeros_like(total)

    def project(e, value):
        total[e, :, :cols] += mm(value, map_ref[0])
        total[e, :, cols:] += mm(value, map_ref[1])

    field[0] = polar_ref[...]
    project(0, polar_ref[...])
    for e in range(1, nodes):
        parent = e ^ (2 ** top_bit(e))
        merged = mm(turn_ref[e - 1], field[parent])
        fine_cos, fine_sin = fine_ref[e - 1, 0], fine_ref[e - 1, 1]
        back = lax.rem(LANES - step * (width // LANES), LANES)
        coarse_cos = pltpu.roll(coarse_ref[e - 1, 0], back, 1)
        coarse_sin = pltpu.roll(coarse_ref[e - 1, 1], back, 1)
        for j in range(width // LANES):
            at = slice(j * LANES, (j + 1) * LANES)
            c = coarse_cos[:, j : j + 1]
            s = coarse_sin[:, j : j + 1]
            cosine = fine_cos * c - fine_sin * s
            sine = fine_cos * s + fine_sin * c
            real, imag = merged[:beams, at], merged[beams:, at]
            field[e, :beams, at] = (real * cosine - imag * sine).astype(BF16)
            field[e, beams:, at] = (real * sine + imag * cosine).astype(BF16)
        project(e, field[e])

    @pl.when(step == pl.num_programs(0) - 1)
    def _():
        for e in range(nodes):
            real = total[e, :beams, :cols] - total[e, beams:, cols:]
            imag = total[e, :beams, cols:] + total[e, beams:, :cols]
            basis = jnp.concatenate([real, imag], axis=0).astype(BF16)
            if e < nodes // 2:
                basis = mm(own_ref[e], basis).astype(BF16)
            out_ref[e] = basis


def tree(polar, range_map, turn, own, fine, coarse, sections, chunk):
    rows, bins = polar.shape
    cols = range_map.shape[2]
    nodes = 2**sections
    whole = lambda array: pl.BlockSpec(array.shape, lambda i: (0,) * array.ndim)
    return pl.pallas_call(
        functools.partial(tree_kernel, sections),
        grid=(bins // chunk,),
        in_specs=[
            pl.BlockSpec((rows, chunk), lambda i: (0, i)),
            pl.BlockSpec((2, chunk, cols), lambda i: (0, i, 0)),
            whole(turn),
            whole(own),
            whole(fine),
            whole(coarse),
        ],
        out_specs=pl.BlockSpec((nodes, rows, cols), lambda i: (0, 0, 0)),
        out_shape=jax.ShapeDtypeStruct((nodes, rows, cols), BF16),
        scratch_shapes=[
            pltpu.VMEM((nodes, rows, chunk), BF16),
            pltpu.VMEM((nodes, rows, 2 * cols), F32),
        ],
        compiler_params=pltpu.CompilerParams(vmem_limit_bytes=52 * 1024 * 1024),
        cost_estimate=pl.CostEstimate(
            flops=40 * 10**9, bytes_accessed=12 * 10**6, transcendentals=0
        ),
        name="tree",
    )(polar, range_map, turn, own, fine, coarse)


def tiles_kernel(slots, place_ref, cover_ref, basis_ref, maps_ref, out_ref):
    e, block = pl.program_id(0), pl.program_id(1)

    @pl.when((e == 0) & (block == 0))
    def _():
        out_ref[...] = jnp.zeros_like(out_ref)

    count, _, rows, beams = maps_ref.shape[1:]
    real = maps_ref[0, :, 0].reshape(count * rows, beams)
    imag = maps_ref[0, :, 1].reshape(count * rows, beams)
    basis = basis_ref[0]
    part_real = mm(jnp.concatenate([real, -imag], axis=1), basis)
    part_imag = mm(jnp.concatenate([imag, real], axis=1), basis)
    first = e * slots + block * count
    for k in range(count):
        tile = cover_ref[first + k]
        out_ref[tile, 0] += part_real[k * rows : (k + 1) * rows]
        out_ref[tile, 1] += part_imag[k * rows : (k + 1) * rows]


def tiles(place, cover, basis, maps, tile_count):
    nodes, slots, _, rows, beams = maps.shape
    block = math.gcd(slots, SLOT_BLOCK)
    cols = basis.shape[2]
    shape = (tile_count, 2, rows, cols)
    return pl.pallas_call(
        functools.partial(tiles_kernel, slots),
        grid_spec=pltpu.PrefetchScalarGridSpec(
            num_scalar_prefetch=2,
            grid=(nodes, slots // block),
            in_specs=[
                pl.BlockSpec((1,) + basis.shape[1:], lambda e, k, p, c: (e, 0, 0)),
                pl.BlockSpec(
                    (1, block, 2, rows, beams), lambda e, k, p, c: (p[0] ^ e, k, 0, 0, 0)
                ),
            ],
            out_specs=pl.BlockSpec(shape, lambda e, k, p, c: (0, 0, 0, 0)),
        ),
        out_shape=jax.ShapeDtypeStruct(shape, F32),
        compiler_params=pltpu.CompilerParams(vmem_limit_bytes=40 * 1024 * 1024),
        cost_estimate=pl.CostEstimate(
            flops=5 * 10**9, bytes_accessed=9 * 10**6, transcendentals=0
        ),
        name="tiles",
    )(place, cover, basis, maps)


def shards(
    raw_echoes,
    chirp_replica,
    steering,
    band_start,
    band_coef,
    phase_rate,
    range_map,
    slot_maps,
    coverage,
):
    pulses, _, range_len = raw_echoes.shape
    tap_count = chirp_replica.shape[1]
    quarter = tap_count // 4
    sections, _, _, _, band, beams = band_coef.shape
    nodes = 2**sections
    subs = lax.axis_size("sub")
    owners = subs * lax.axis_size("rng")
    slot_count = slot_maps.shape[0]
    bins = range_len // 2
    groups = None
    if subs != nodes:
        groups = [list(range(g, g + nodes)) for g in range(0, subs, nodes)]
    place = lax.axis_index("sub") % nodes

    everywhere = (sections, 2, 1, beams)
    cover_row = jnp.pad(coverage[:, 0].astype(F32), (0, beams - slot_count))
    packed = jnp.concatenate(
        [
            band_coef[:, 0].astype(F32).reshape(sections, 2, 2 * band, beams),
            band_start[:, 0].astype(F32)[:, :, None],
            jnp.broadcast_to(phase_rate[:, 0][:, None, None], everywhere),
            jnp.broadcast_to(cover_row, everywhere),
        ],
        axis=2,
    )
    relative = packed[None]
    for bit in reversed(range(sections)):
        relative = jnp.concatenate([relative, swapped(relative, "sub", bit)], axis=0)
    spot = [sum(((e >> b) & 1) << (sections - 1 - b) for b in range(sections)) for e in range(nodes)]
    maps = lax.all_gather(slot_maps, "sub", axis_index_groups=groups)
    cover = jnp.concatenate([relative[n, 0, 0, 2 * band + 2, :slot_count] for n in spot])
    cover = cover.astype(jnp.int32)
    turn, own = matrices(relative, spot, sections, band)
    rate = jnp.stack(
        [relative[spot[e], top_bit(e), 1, 2 * band + 1] for e in range(1, nodes)]
    )
    unit = 2.0 * math.pi / bins
    lane = lax.iota(jnp.int32, LANES).astype(F32)
    chunk = 512
    first = (
        lax.axis_index("rng") * bins + lax.iota(jnp.int32, LANES) * LANES
    ).astype(F32)
    fine_angle = rate[:, :, None] * lane * unit
    fine = jnp.stack([jnp.cos(fine_angle), jnp.sin(fine_angle)], axis=1)
    coarse_angle = rate[:, :, None] * first * unit
    coarse = jnp.stack([jnp.cos(coarse_angle), jnp.sin(coarse_angle)], axis=1)

    raw = raw_echoes.reshape(2 * pulses, range_len)
    halo = from_behind(raw_echoes[:, :, :tap_count], "rng", -1).reshape(2 * pulses, tap_count)
    taps = toeplitz_taps(chirp_replica, quarter, 6 * quarter)
    taps = taps.reshape(6 * quarter, 2 * quarter)
    real, imag = steering[0, 0], steering[0, 1]
    steer = jnp.concatenate(
        [
            jnp.stack([real, -imag], axis=2).reshape(beams, 2 * pulses),
            jnp.stack([imag, real], axis=2).reshape(beams, 2 * pulses),
        ],
        axis=0,
    )
    polar = front(steer, taps, raw, halo)
    basis = tree(polar, range_map, turn, own, fine, coarse, sections, chunk)
    partial = tiles(place.reshape(1), cover, basis, maps, owners)
    cores = lax.axis_size("rng")
    partial = partial.reshape((subs, cores) + partial.shape[1:])
    core = lax.axis_index("rng")
    half = lax.dynamic_index_in_dim(partial, core, 1, keepdims=False)
    for step in range(1, cores):
        away = lax.dynamic_index_in_dim(partial, (core + step) % cores, 1, keepdims=False)
        pairs = [(c, (c + step) % cores) for c in range(cores)]
        half = half + lax.ppermute(away.astype(BF16), "rng", pairs).astype(F32)
    received = lax.all_to_all(half.astype(BF16), "sub", split_axis=0, concat_axis=0, tiled=True)
    return jnp.sum(received.astype(F32), axis=0, keepdims=True)


def solution(mesh):
    in_specs = (
        P("sub", None, "rng"),
        P(),
        P("sub", None, None, None),
        P(None, "sub", None, None),
        P(None, "sub", None, None, None, None),
        P(None, "sub", None),
        P(None, "rng", None),
        P(("sub", "rng"), None, None, None),
        P(("sub", "rng"), None),
    )
    out_specs = P(("sub", "rng"), None, None, None)
    return jax.shard_map(shards, mesh=mesh, in_specs=in_specs, out_specs=out_specs, check_vma=False)
```
